256 devices in a mesh: seq: 32 (over z_lo, x, y), head: 8 (over z_hi, core).
Axes of the slice: x: 4, y: 4, z: 8 (z_hi: 4, z_lo: 2; z = z_hi * 2 + z_lo), core: 2. Of those that a mesh axis runs over, the one named last changes fastest.
Arguments:
- query_tokens: bfloat16 [40960, 3072], P(('seq', 'head')), may hold values from -6 to 6
- key_tokens: bfloat16 [40960, 3072], P(('seq', 'head')), may hold values from -6 to 6
- value_tokens: bfloat16 [40960, 3072], P(('seq', 'head')), may hold values from -6 to 6
- matching: int32 [2, 32], replicated, may hold values from 0 to 31, as said below
Outputs:
- attended: bfloat16 [40960, 3072], P(('seq', 'head'))
The draws below stay inside these ranges and needn't reach their ends.
Inputs may be any that keep to these rules, and one draw needn't show every extreme that they name: For each round r and block b: matching[r, matching[r, b]] == b and matching[r, b] != b; the 2 rows give every block different partners.
All inputs are finite; a program needn't handle non-finite values.
Results may differ from the reference program's by a relative error of at most 0.0048.
Values may be sent and summed in bfloat16 or wider, within the bound.
A program may use at most 64 MiB of HBM per device.

```python
import jax
import jax.numpy as jnp
from jax import lax

HEADS = 24
HEAD_DIM = 128
WIDTH = 3072
ROUNDS = 2
BLOCKS = 32
BLOCK_TOK = 1280
TOKENS = 40960


def drawn_pair(key):
    query_base = jnp.clip(jax.random.normal(jax.random.fold_in(key, 21), (TOKENS, WIDTH), jnp.float32), -6.0, 6.0)
    key_base = jnp.clip(jax.random.normal(jax.random.fold_in(key, 22), (TOKENS, WIDTH), jnp.float32), -6.0, 6.0)
    return (query_base, key_base)


def draw_query_tokens(key, part):
    return drawn_pair(jax.random.fold_in(key, 5))[0].astype(jnp.bfloat16)


def draw_key_tokens(key, part):
    return drawn_pair(jax.random.fold_in(key, 5))[1].astype(jnp.bfloat16)


def draw_matching(key, part):
    count = BLOCKS
    relabel = jax.random.permutation(jax.random.fold_in(key, 31), count).astype(jnp.int32)
    first_round = jax.random.randint(jax.random.fold_in(key, 32), (), 0, count - 1)
    second_round = (first_round + jax.random.randint(jax.random.fold_in(key, 33), (), 1, count - 1)) % (count - 1)
    players = jnp.arange(count, dtype=jnp.int32)

    def circle(turn):
        other = (2 * turn - players) % (count - 1)
        base = jnp.where(players == count - 1, turn, jnp.where(players == turn, count - 1, other))
        return jnp.zeros((count,), jnp.int32).at[relabel].set(relabel[base])
    return jnp.stack([circle(first_round), circle(second_round)]).astype(jnp.int32)


def levels(key, dims, pieces, least, top_value):
    gain = 1.0
    for position, parts in pieces:
        heights = jax.random.uniform(jax.random.fold_in(jax.random.fold_in(key, 6), position), (parts,), jnp.float32, least / len(pieces), top_value / len(pieces))
        gain = gain * jnp.repeat(jnp.exp(heights), dims[position] // parts).reshape((-1,) + (1,) * (len(dims) - 1 - position))
    return gain


def scatter_about(stream_key, extent, width, bound, split=(), kind=jnp.bfloat16):
    values = jax.random.normal(stream_key, extent, jnp.float32) * width
    if len(split) > 0:
        values = levels(stream_key, extent, split, -0.22, 0.18) * values
    return jnp.clip(values, min=-bound, max=bound).astype(kind)


def setup_inputs(seed: int = 0) -> dict:
    splits = jax.random.split(jax.random.key(seed), 5)
    return {
        "query_tokens": draw_query_tokens(jax.random.fold_in(splits[4], 71), 0),
        "key_tokens": draw_key_tokens(jax.random.fold_in(splits[4], 71), 0),
        "value_tokens": scatter_about(splits[2], (TOKENS, WIDTH), 1.0, 6.0, ((0, 256),)),
        "matching": draw_matching(jax.random.fold_in(splits[4], 71), 0),
    }


def reference(query_tokens, key_tokens, value_tokens, matching):
    query_blocks = query_tokens.reshape(BLOCKS, BLOCK_TOK, WIDTH)
    key_blocks = key_tokens.reshape(BLOCKS, BLOCK_TOK, WIDTH)
    value_blocks = value_tokens.reshape(BLOCKS, BLOCK_TOK, WIDTH)
    score_scale = 1.0 / (HEAD_DIM ** 0.5)

    def one_block(index):
        key_list = [key_blocks[index]]
        value_list = [value_blocks[index]]
        for round_index in range(ROUNDS):
            partner = matching[round_index, index]
            key_list.append(key_blocks[partner])
            value_list.append(value_blocks[partner])
        key_rows = jnp.concatenate(key_list, 0).astype(jnp.float32).reshape(-1, HEADS, HEAD_DIM)
        value_rows = jnp.concatenate(value_list, 0).astype(jnp.float32).reshape(-1, HEADS, HEAD_DIM)
        query_rows = query_blocks[index].astype(jnp.float32).reshape(BLOCK_TOK, HEADS, HEAD_DIM)
        scores = jnp.einsum("qhd,khd->hqk", query_rows, key_rows) * score_scale
        weights = jnp.exp(scores - jnp.max(scores, axis=-1, keepdims=True))
        totals = jnp.sum(weights, axis=-1)
        rounded = weights.astype(jnp.bfloat16).astype(jnp.float32)
        mixed = jnp.einsum("hqk,khd->qhd", rounded, value_rows)
        result = mixed / jnp.transpose(totals)[:, :, None]
        return result.reshape(BLOCK_TOK, WIDTH).astype(jnp.bfloat16)

    attended = lax.map(one_block, jnp.arange(BLOCKS, dtype=jnp.int32))
    return attended.reshape(TOKENS, WIDTH)
```

```python
import math

import jax
import jax.numpy as jnp
from jax import lax
from jax.experimental import pallas as pl
from jax.experimental.pallas import tpu as pltpu
from jax.sharding import PartitionSpec as P

HEAD_DIM = 128
ROUNDS = 2
BLOCKS = 32
BLOCK_TOK = 1280
SHARD_TOK = 160
WIDTH = 3072
LEVELS = 8
SIDE = 4
PLANE = SIDE * SIDE
GROUP = WIDTH // HEAD_DIM // LEVELS
PIECE = BLOCK_TOK // PLANE
TILE = 256
EXP2_SCALE = math.log2(math.e) / math.sqrt(HEAD_DIM)
MESH = pl.DeviceIdType.MESH
KEY, VALUE, QUERY = range(3)


def rows(start, size, step=None):
    return pl.ds(pl.multiple_of(start, step or size), size)


def attend_chunk(query, keys, values, before=None):
    scores = lax.dot_general(query, keys, (((1,), (1,)), ((), ())), preferred_element_type=jnp.float32)
    largest = jnp.max(scores, axis=-1, keepdims=True)
    if before is not None:
        largest = jnp.maximum(largest, before[0])
    weights = jnp.exp2((scores - largest) * EXP2_SCALE)
    totals = jnp.sum(weights, axis=-1, keepdims=True)
    mixed = jnp.dot(weights.astype(jnp.bfloat16), values, preferred_element_type=jnp.float32)
    if before is not None:
        shrink = jnp.exp2((before[0] - largest) * EXP2_SCALE)
        totals += before[1] * shrink
        mixed += before[2] * shrink
    return largest, totals, mixed


def kernel(match_ref, query_ref, key_ref, value_ref, out_ref, *scratch):
    (shards, near, query, largest, totals, mixed, done) = scratch[:7]
    spread, stage, partner = scratch[7:10], scratch[10:13], scratch[13:16]
    load_sem, send_sem, near_sem, spread_send, spread_sem, partner_send, partner_sem, out_send, out_sem = scratch[16:]

    seq, head = lax.axis_index("seq"), lax.axis_index("head")
    z_low, chip = lax.div(seq, PLANE), lax.rem(seq, PLANE)
    z_high, core = lax.div(head, 2), lax.rem(head, 2)
    x, y = lax.div(chip, SIDE), lax.rem(chip, SIDE)
    level = z_high * 2 + z_low
    block = core * PLANE + chip

    def column_device(at_level, at_core):
        return lax.rem(at_level, 2) * PLANE + chip, lax.div(at_level, 2) * 2 + at_core

    def plane_device(at_chip, at_core):
        return z_low * PLANE + at_chip, z_high * 2 + at_core

    def plane_chip(step):
        across = lax.rem(step, SIDE)
        down = lax.rem(lax.div(step, SIDE) + across, SIDE)
        return lax.rem(x + across, SIDE) * SIDE + lax.rem(y + down, SIDE)

    def put(source, target, send, recv, device):
        here = jnp.logical_and(device[0] == seq, device[1] == head)

        @pl.when(here)
        def _():
            pltpu.make_async_copy(source, target, recv).start()

        @pl.when(jnp.logical_not(here))
        def _():
            pltpu.make_async_remote_copy(source, target, send, recv, device_id=device, device_id_type=MESH).start()

    def wait_bytes(ref, sem):
        pltpu.make_async_copy(ref, ref, sem).wait()

    for array, ref in ((KEY, key_ref), (VALUE, value_ref), (QUERY, query_ref)):
        pltpu.make_async_copy(ref, shards.at[array], load_sem.at[array]).start()

    barrier = pltpu.get_barrier_semaphore()

    def greet_column(step, carry):
        device = column_device(lax.rem(level + lax.div(step, 2), LEVELS), lax.rem(core + lax.rem(step, 2), 2))
        pl.semaphore_signal(barrier, inc=1, device_id=device, device_id_type=MESH)
        return carry

    def greet_plane(step, carry):
        device = plane_device(plane_chip(lax.div(step, 2)), lax.rem(step, 2))
        pl.semaphore_signal(barrier, inc=1, device_id=device, device_id_type=MESH)
        return carry

    lax.fori_loop(1, 2 * LEVELS, greet_column, 0)
    lax.fori_loop(2, 2 * PLANE, greet_plane, 0)
    pl.semaphore_wait(barrier, 2 * LEVELS + 2 * PLANE - 3)

    def near_target(array, index):
        return query.at[index] if array == QUERY else near.at[index, array]

    def send_near(index, array):
        def one(step, carry):
            sign = 1 - 2 * lax.rem(step, 2)
            to = lax.rem(level + LEVELS // 2 + sign * lax.div(step + 1, 2), LEVELS)
            put(
                shards.at[array, :, rows((to * GROUP + index) * HEAD_DIM, HEAD_DIM)],
                near_target(array, index).at[rows(head * SHARD_TOK, SHARD_TOK)],
                send_sem.at[index, array],
                near_sem.at[index, array],
                column_device(to, z_low),
            )
            return carry

        lax.fori_loop(0, LEVELS, one, 0)

    def wait_near(index, array):
        wait_bytes(near_target(array, index), near_sem.at[index, array])

    def send_spread(index, at_core):
        def one(step, carry):
            to = plane_chip(step)
            put(
                near.at[index, at_core, rows(to * PIECE, PIECE)],
                spread[index].at[block],
                spread_send.at[index],
                spread_sem.at[index],
                plane_device(to, at_core),
            )
            return carry

        lax.fori_loop(0, PLANE, one, 0)

    def send_partner(index):
        wait_bytes(spread[index], spread_sem.at[index])

        def one(step, carry):
            to, at_core = plane_chip(lax.div(step, 2)), lax.rem(step, 2)
            owner = at_core * PLANE + to
            for round_index in range(ROUNDS):
                stage[index][owner, round_index * PIECE : (round_index + 1) * PIECE, :] = spread[index][
                    match_ref[round_index, owner]
                ]
            put(
                stage[index].at[owner],
                partner[index].at[core, chip],
                partner_send.at[index],
                partner_sem.at[index],
                plane_device(to, at_core),
            )
            return carry

        lax.fori_loop(0, BLOCKS, one, 0)

    def attend_near(index):
        def one(step, carry):
            at = rows(step * TILE, TILE)
            found = attend_chunk(query[index, at], near[index, KEY], near[index, VALUE])
            largest[index, at], totals[index, at], mixed[index, at] = found
            return carry

        lax.fori_loop(0, BLOCK_TOK // TILE, one, 0)

    def attend_partner(index):
        wait_bytes(partner[index], partner_sem.at[index])
        keys = partner[index].at[KEY]
        values = partner[index].at[VALUE]

        def one(step, carry):
            at = rows(step * TILE, TILE)
            _, sums, found = attend_chunk(
                query[index, at],
                keys[...].reshape(ROUNDS * BLOCK_TOK, HEAD_DIM),
                values[...].reshape(ROUNDS * BLOCK_TOK, HEAD_DIM),
                (largest[index, at], totals[index, at], mixed[index, at]),
            )
            done[index, at] = (found / sums).astype(jnp.bfloat16)
            return carry

        lax.fori_loop(0, BLOCK_TOK // TILE, one, 0)

        def give(step, carry):
            to = lax.rem(head + step, LEVELS)
            put(
                done.at[index, rows(to * SHARD_TOK, SHARD_TOK)],
                out_ref.at[:, rows((level * GROUP + index) * HEAD_DIM, HEAD_DIM)],
                out_send.at[index],
                out_sem,
                (block, to),
            )
            return carry

        lax.fori_loop(0, LEVELS, give, 0)

    for array in (KEY, VALUE, QUERY):
        wait_bytes(shards.at[array], load_sem.at[array])
    for index in range(GROUP):
        for array in (KEY, VALUE, QUERY):
            send_near(index, array)

    def spread_both(index):
        for array in (KEY, VALUE):
            wait_near(index, array)
            send_spread(index, array)

    spread_both(0)
    wait_near(0, QUERY)
    attend_near(0)
    send_partner(0)
    spread_both(1)
    wait_near(1, QUERY)
    attend_near(1)
    send_partner(1)
    attend_partner(0)
    spread_both(2)
    send_partner(2)
    wait_near(2, QUERY)
    attend_near(2)
    attend_partner(1)
    attend_partner(2)

    own = core == z_low

    for index in range(GROUP):
        for array in (KEY, VALUE, QUERY):
            @pl.when(own)
            def _():
                wait_bytes(query.at[index, pl.ds(0, (LEVELS - 1) * SHARD_TOK)], send_sem.at[index, array])

            @pl.when(jnp.logical_not(own))
            def _():
                wait_bytes(query.at[index], send_sem.at[index, array])

        wait_bytes(spread[index].at[pl.ds(0, BLOCKS - 1)], spread_send.at[index])
        wait_bytes(stage[index].at[pl.ds(0, BLOCKS - 1)], partner_send.at[index])

        @pl.when(own)
        def _():
            wait_bytes(done.at[index, pl.ds(0, (LEVELS - 1) * SHARD_TOK)], out_send.at[index])

        @pl.when(jnp.logical_not(own))
        def _():
            wait_bytes(done.at[index], out_send.at[index])

    wait_bytes(out_ref, out_sem)


def per_device(query_tokens, key_tokens, value_tokens, matching):
    whole = pl.BlockSpec(memory_space=pl.ANY)
    bf16, f32 = jnp.bfloat16, jnp.float32
    return pl.pallas_call(
        kernel,
        out_shape=jax.ShapeDtypeStruct(query_tokens.shape, bf16),
        in_specs=[pl.BlockSpec(memory_space=pltpu.SMEM), whole, whole, whole],
        out_specs=whole,
        scratch_shapes=[
            pltpu.VMEM((3, SHARD_TOK, WIDTH), bf16),
            pltpu.VMEM((GROUP, 2, BLOCK_TOK, HEAD_DIM), bf16),
            pltpu.VMEM((GROUP, BLOCK_TOK, HEAD_DIM), bf16),
            pltpu.VMEM((GROUP, BLOCK_TOK, 1), f32),
            pltpu.VMEM((GROUP, BLOCK_TOK, 1), f32),
            pltpu.VMEM((GROUP, BLOCK_TOK, HEAD_DIM), f32),
            pltpu.VMEM((GROUP, BLOCK_TOK, HEAD_DIM), bf16),
            *[pltpu.VMEM((BLOCKS, PIECE, HEAD_DIM), bf16)] * GROUP,
            *[pltpu.VMEM((BLOCKS, ROUNDS * PIECE, HEAD_DIM), bf16)] * GROUP,
            *[pltpu.VMEM((2, PLANE, ROUNDS * PIECE, HEAD_DIM), bf16)] * GROUP,
            pltpu.SemaphoreType.DMA((3,)),
            pltpu.SemaphoreType.DMA((GROUP, 3)),
            pltpu.SemaphoreType.DMA((GROUP, 3)),
            pltpu.SemaphoreType.DMA((GROUP,)),
            pltpu.SemaphoreType.DMA((GROUP,)),
            pltpu.SemaphoreType.DMA((GROUP,)),
            pltpu.SemaphoreType.DMA((GROUP,)),
            pltpu.SemaphoreType.DMA((GROUP,)),
            pltpu.SemaphoreType.DMA,
        ],
        compiler_params=pltpu.CompilerParams(
            collective_id=0, has_side_effects=True, vmem_limit_bytes=56 * 2**20
        ),
    )(matching, query_tokens, key_tokens, value_tokens)


def solution(mesh):
    return jax.shard_map(
        per_device,
        mesh=mesh,
        in_specs=(
            P(("seq", "head"), None),
            P(("seq", "head"), None),
            P(("seq", "head"), None),
            P(),
        ),
        out_specs=P(("seq", "head"), None),
        check_vma=False,
    )
```

```python
import functools
import math

import jax
import jax.numpy as jnp
from jax import lax
from jax.experimental import pallas as pl
from jax.experimental.pallas import tpu as pltpu
from jax.sharding import PartitionSpec as P

HEAD_DIM = 128
ROUNDS = 2
BLOCKS = 32
BLOCK_TOK = 1280
SHARD_TOK = 160
WIDTH = 3072
LEVELS = 8
SIDE = 4
PLANE = SIDE * SIDE
GROUP = WIDTH // HEAD_DIM // LEVELS
PIECE = BLOCK_TOK // PLANE
CHUNK = 256
EXP2_SCALE = math.log2(math.e) / math.sqrt(HEAD_DIM)
MESH = pl.DeviceIdType.MESH
KEY, VALUE, QUERY = range(3)
NEAR_ORDER = (
    (KEY, 0),
    (VALUE, 0),
    (QUERY, 0),
    (KEY, 1),
    (VALUE, 1),
    (KEY, 2),
    (VALUE, 2),
    (QUERY, 1),
    (QUERY, 2),
)
ROUND_SETS = (((0, 1),), ((0, 1),), ((0,), (1,)))
PARTS = (1, 1, 2)


def rows(start, size, step=None):
    return pl.ds(pl.multiple_of(start, step or size), size)


def attend_chunks(query, pairs, before=None):
    scores = [
        lax.dot_general(keys, query, (((1,), (1,)), ((), ())), preferred_element_type=jnp.float32)
        for keys, _ in pairs
    ]
    largest = functools.reduce(jnp.maximum, [jnp.max(part, axis=0, keepdims=True) for part in scores])
    if before is not None:
        largest = jnp.maximum(largest, before[0])
    totals, mixed = 0.0, 0.0
    for part, (_, values) in zip(scores, pairs):
        weights = jnp.exp2((part - largest) * EXP2_SCALE)
        totals += jnp.sum(weights, axis=0, keepdims=True)
        mixed += jnp.dot(values, weights.astype(jnp.bfloat16), preferred_element_type=jnp.float32)
    if before is not None:
        shrink = jnp.exp2((before[0] - largest) * EXP2_SCALE)
        totals += before[1] * shrink
        mixed += before[2] * shrink
    return largest, totals, mixed


def kernel(match_ref, query_ref, key_ref, value_ref, out_ref, *scratch):
    (shards, near, query, largest, totals, mixed, done, turned) = scratch[:8]
    spread, stage, partner = scratch[8:11], scratch[11:14], scratch[14:17]
    load_sem, send_sem, near_sem, spread_send, spread_sem, partner_send, partner_sem, out_send, out_sem = scratch[17:]

    seq, head = lax.axis_index("seq"), lax.axis_index("head")
    z_low, chip = lax.div(seq, PLANE), lax.rem(seq, PLANE)
    z_high, core = lax.div(head, 2), lax.rem(head, 2)
    x, y = lax.div(chip, SIDE), lax.rem(chip, SIDE)
    level = z_high * 2 + z_low
    block = core * PLANE + chip

    def column_device(at_level, at_core):
        return lax.rem(at_level, 2) * PLANE + chip, lax.div(at_level, 2) * 2 + at_core

    def plane_device(at_chip, at_core):
        return z_low * PLANE + at_chip, z_high * 2 + at_core

    def plane_chip(step):
        across = lax.rem(step, SIDE)
        down = lax.rem(lax.div(step, SIDE) + across, SIDE)
        return lax.rem(x + across, SIDE) * SIDE + lax.rem(y + down, SIDE)

    def put(source, target, send, recv, device):
        here = jnp.logical_and(device[0] == seq, device[1] == head)

        @pl.when(here)
        def _():
            pltpu.make_async_copy(source, target, recv).start()

        @pl.when(jnp.logical_not(here))
        def _():
            pltpu.make_async_remote_copy(source, target, send, recv, device_id=device, device_id_type=MESH).start()

    def wait_bytes(ref, sem):
        pltpu.make_async_copy(ref, ref, sem).wait()

    for array, ref in ((KEY, key_ref), (VALUE, value_ref), (QUERY, query_ref)):
        pltpu.make_async_copy(ref, shards.at[array], load_sem.at[array]).start()

    barrier = pltpu.get_barrier_semaphore()

    def greet_column(step, carry):
        device = column_device(lax.rem(level + lax.div(step, 2), LEVELS), lax.rem(core + lax.rem(step, 2), 2))
        pl.semaphore_signal(barrier, inc=1, device_id=device, device_id_type=MESH)
        return carry

    def greet_plane(step, carry):
        device = plane_device(plane_chip(lax.div(step, 2)), lax.rem(step, 2))
        pl.semaphore_signal(barrier, inc=1, device_id=device, device_id_type=MESH)
        return carry

    lax.fori_loop(1, 2 * LEVELS, greet_column, 0)
    lax.fori_loop(2, 2 * PLANE, greet_plane, 0)
    pl.semaphore_wait(barrier, 2 * LEVELS + 2 * PLANE - 3)

    def near_target(array, index):
        return query.at[index] if array == QUERY else near.at[index, array]

    def send_near(index, array):
        def one(step, carry):
            sign = 1 - 2 * lax.rem(step, 2)
            to = lax.rem(level + LEVELS // 2 + sign * lax.div(step + 1, 2), LEVELS)
            put(
                shards.at[array, :, rows((to * GROUP + index) * HEAD_DIM, HEAD_DIM)],
                near_target(array, index).at[rows(head * SHARD_TOK, SHARD_TOK)],
                send_sem.at[index, array],
                near_sem.at[index, array],
                column_device(to, z_low),
            )
            return carry

        lax.fori_loop(0, LEVELS, one, 0)

    def wait_near(index, array):
        wait_bytes(near_target(array, index), near_sem.at[index, array])

    def send_spread(index, at_core):
        def one(step, carry):
            to = plane_chip(step)
            put(
                near.at[index, at_core, rows(to * PIECE, PIECE)],
                spread[index].at[block],
                spread_send.at[index],
                spread_sem.at[index],
                plane_device(to, at_core),
            )
            return carry

        lax.fori_loop(0, PLANE, one, 0)

    def send_partner(index):
        wait_bytes(spread[index], spread_sem.at[index])
        for rounds in ROUND_SETS[index]:

            def one(step, carry):
                to, at_core = plane_chip(lax.div(step, 2)), lax.rem(step, 2)
                owner = at_core * PLANE + to
                for round_index in rounds:
                    stage[index][round_index, owner] = spread[index][match_ref[round_index, owner]]
                span = pl.ds(rounds[0], len(rounds))
                put(
                    stage[index].at[span, owner],
                    partner[index].at[span, core, rows(chip * PIECE, PIECE)],
                    partner_send.at[index, rounds[0]],
                    partner_sem.at[index, rounds[0]],
                    plane_device(to, at_core),
                )
                return carry

            lax.fori_loop(0, BLOCKS, one, 0)

    def chunks(ref, turned):
        spans = [slice(start, start + CHUNK) for start in range(0, BLOCK_TOK, CHUNK)]
        return [(ref[KEY, span], turned[:, span]) for span in spans]

    def keep(index, found):
        largest[index], totals[index], mixed[index] = found

    def attend_near(index):
        turned[0] = near[index, VALUE].T
        keep(index, attend_chunks(query[index], chunks(near.at[index], turned.at[0])))

    def attend_partner(index, rounds):
        wait_bytes(partner[index].at[pl.ds(rounds[0], len(rounds))], partner_sem.at[index, rounds[0]])
        pairs = []
        for round_index in rounds:
            turned[round_index] = partner[index][round_index, VALUE].T
            pairs += chunks(partner[index].at[round_index], turned.at[round_index])
        last = rounds[-1] == ROUNDS - 1
        parts = PARTS[index] if last else 1
        width = BLOCK_TOK // parts
        for part in range(parts):
            at = slice(part * width, (part + 1) * width)
            before = largest[index, :, at], totals[index, :, at], mixed[index, :, at]
            found = attend_chunks(query[index, at], pairs, before)
            if not last:
                keep(index, found)
                continue
            done[index, at] = (found[2] / found[1]).T.astype(jnp.bfloat16)
            give(index, part * LEVELS // parts, (part + 1) * LEVELS // parts)

    def give(index, first, end):
        def one(to, carry):
            put(
                done.at[index, rows(to * SHARD_TOK, SHARD_TOK)],
                out_ref.at[:, rows((level * GROUP + index) * HEAD_DIM, HEAD_DIM)],
                out_send.at[index],
                out_sem,
                (block, to),
            )
            return carry

        lax.fori_loop(first, end, one, 0)

    for array in (KEY, VALUE, QUERY):
        wait_bytes(shards.at[array], load_sem.at[array])
    for array, index in NEAR_ORDER:
        send_near(index, array)

    def spread_one(index, array):
        wait_near(index, array)
        send_spread(index, array)

    def near_part(index):
        wait_near(index, QUERY)
        attend_near(index)

    spread_one(0, KEY)
    spread_one(0, VALUE)
    send_partner(0)
    near_part(0)
    spread_one(1, KEY)
    spread_one(1, VALUE)
    send_partner(1)
    attend_partner(0, (0, 1))
    spread_one(2, KEY)
    spread_one(2, VALUE)
    near_part(1)
    send_partner(2)
    attend_partner(1, (0, 1))
    near_part(2)
    attend_partner(2, (0,))
    attend_partner(2, (1,))

    own = core == z_low

    for index in range(GROUP):
        for array in (KEY, VALUE, QUERY):
            @pl.when(own)
            def _():
                wait_bytes(query.at[index, pl.ds(0, (LEVELS - 1) * SHARD_TOK)], send_sem.at[index, array])

            @pl.when(jnp.logical_not(own))
            def _():
                wait_bytes(query.at[index], send_sem.at[index, array])

        wait_bytes(spread[index].at[pl.ds(0, BLOCKS - 1)], spread_send.at[index])
        for rounds in ROUND_SETS[index]:
            wait_bytes(stage[index].at[pl.ds(rounds[0], len(rounds)), pl.ds(0, BLOCKS - 1)], partner_send.at[index, rounds[0]])

        @pl.when(own)
        def _():
            wait_bytes(done.at[index, pl.ds(0, (LEVELS - 1) * SHARD_TOK)], out_send.at[index])

        @pl.when(jnp.logical_not(own))
        def _():
            wait_bytes(done.at[index], out_send.at[index])

    wait_bytes(out_ref, out_sem)


def per_device(query_tokens, key_tokens, value_tokens, matching):
    whole = pl.BlockSpec(memory_space=pl.ANY)
    bf16, f32 = jnp.bfloat16, jnp.float32
    return pl.pallas_call(
        kernel,
        out_shape=jax.ShapeDtypeStruct(query_tokens.shape, bf16),
        in_specs=[pl.BlockSpec(memory_space=pltpu.SMEM), whole, whole, whole],
        out_specs=whole,
        scratch_shapes=[
            pltpu.VMEM((3, SHARD_TOK, WIDTH), bf16),
            pltpu.VMEM((GROUP, 2, BLOCK_TOK, HEAD_DIM), bf16),
            pltpu.VMEM((GROUP, BLOCK_TOK, HEAD_DIM), bf16),
            pltpu.VMEM((GROUP, 1, BLOCK_TOK), f32),
            pltpu.VMEM((GROUP, 1, BLOCK_TOK), f32),
            pltpu.VMEM((GROUP, HEAD_DIM, BLOCK_TOK), f32),
            pltpu.VMEM((GROUP, BLOCK_TOK, HEAD_DIM), bf16),
            pltpu.VMEM((ROUNDS, HEAD_DIM, BLOCK_TOK), bf16),
            *[pltpu.VMEM((BLOCKS, PIECE, HEAD_DIM), bf16)] * GROUP,
            *[pltpu.VMEM((ROUNDS, BLOCKS, PIECE, HEAD_DIM), bf16)] * GROUP,
            *[pltpu.VMEM((ROUNDS, 2, BLOCK_TOK, HEAD_DIM), bf16)] * GROUP,
            pltpu.SemaphoreType.DMA((3,)),
            pltpu.SemaphoreType.DMA((GROUP, 3)),
            pltpu.SemaphoreType.DMA((GROUP, 3)),
            pltpu.SemaphoreType.DMA((GROUP,)),
            pltpu.SemaphoreType.DMA((GROUP,)),
            pltpu.SemaphoreType.DMA((GROUP, ROUNDS)),
            pltpu.SemaphoreType.DMA((GROUP, ROUNDS)),
            pltpu.SemaphoreType.DMA((GROUP,)),
            pltpu.SemaphoreType.DMA,
        ],
        compiler_params=pltpu.CompilerParams(
            collective_id=0, has_side_effects=True, vmem_limit_bytes=56 * 2**20
        ),
    )(matching, query_tokens, key_tokens, value_tokens)


def solution(mesh):
    return jax.shard_map(
        per_device,
        mesh=mesh,
        in_specs=(
            P(("seq", "head"), None),
            P(("seq", "head"), None),
            P(("seq", "head"), None),
            P(),
        ),
        out_specs=P(("seq", "head"), None),
        check_vma=False,
    )
```

```python
import functools
import math

import jax
import jax.numpy as jnp
from jax import lax
from jax.experimental import pallas as pl
from jax.experimental.pallas import tpu as pltpu
from jax.sharding import PartitionSpec as P

HEAD_DIM = 128
ROUNDS = 2
BLOCKS = 32
BLOCK_TOK = 1280
SHARD_TOK = 160
WIDTH = 3072
LEVELS = 8
SIDE = 4
PLANE = SIDE * SIDE
GROUP = WIDTH // HEAD_DIM // LEVELS
PIECE = BLOCK_TOK // PLANE
CHUNK = 256
EXP2_SCALE = math.log2(math.e) / math.sqrt(HEAD_DIM)
MESH = pl.DeviceIdType.MESH
KEY, VALUE, QUERY = range(3)
ROUND_SETS = (((0, 1),), ((0, 1),), ((0,), (1,)))
PARTS = (1, 1, 2)


def rows(start, size, step=None):
    return pl.ds(pl.multiple_of(start, step or size), size)


def attend_chunks(query, pairs, before=None):
    scores = [
        lax.dot_general(keys, query, (((1,), (1,)), ((), ())), preferred_element_type=jnp.float32)
        for keys, _ in pairs
    ]
    largest = functools.reduce(jnp.maximum, [jnp.max(part, axis=0, keepdims=True) for part in scores])
    if before is not None:
        largest = jnp.maximum(largest, before[0])
    totals, mixed = 0.0, 0.0
    for part, (_, values) in zip(scores, pairs):
        weights = jnp.exp2((part - largest) * EXP2_SCALE)
        totals += jnp.sum(weights, axis=0, keepdims=True)
        mixed += jnp.dot(values, weights.astype(jnp.bfloat16), preferred_element_type=jnp.float32)
    if before is not None:
        shrink = jnp.exp2((before[0] - largest) * EXP2_SCALE)
        totals += before[1] * shrink
        mixed += before[2] * shrink
    return largest, totals, mixed


def kernel(match_ref, query_ref, key_ref, value_ref, out_ref, *scratch):
    (shards, near, query, largest, totals, mixed, done, turned) = scratch[:8]
    spread, stage, partner = scratch[8:11], scratch[11:14], scratch[14:17]
    load_sem, send_sem, near_sem, spread_send, spread_sem, partner_send, partner_sem, out_send, out_sem, line_sem, core_sem = scratch[17:]

    seq, head = lax.axis_index("seq"), lax.axis_index("head")
    z_low, chip = lax.div(seq, PLANE), lax.rem(seq, PLANE)
    z_high, core = lax.div(head, 2), lax.rem(head, 2)
    x, y = lax.div(chip, SIDE), lax.rem(chip, SIDE)
    level = z_high * 2 + z_low
    block = core * PLANE + chip

    def column_device(at_level, at_core):
        return lax.rem(at_level, 2) * PLANE + chip, lax.div(at_level, 2) * 2 + at_core

    def plane_device(at_chip, at_core):
        return z_low * PLANE + at_chip, z_high * 2 + at_core

    def plane_chip(step):
        across = lax.rem(lax.div(step, SIDE) + step, SIDE)
        down = lax.rem(step * 3 + lax.div(step, SIDE) * 2, SIDE)
        return lax.rem(x + across, SIDE) * SIDE + lax.rem(y + down, SIDE)

    def put(source, target, send, recv, device):
        here = jnp.logical_and(device[0] == seq, device[1] == head)

        @pl.when(here)
        def _():
            pltpu.make_async_copy(source, target, recv).start()

        @pl.when(jnp.logical_not(here))
        def _():
            pltpu.make_async_remote_copy(source, target, send, recv, device_id=device, device_id_type=MESH).start()

    def wait_bytes(ref, sem):
        pltpu.make_async_copy(ref, ref, sem).wait()

    for array, ref in ((KEY, key_ref), (VALUE, value_ref), (QUERY, query_ref)):
        pltpu.make_async_copy(ref, shards.at[array], load_sem.at[array]).start()

    barrier = pltpu.get_barrier_semaphore()

    def greet_column(step, carry):
        device = column_device(lax.rem(level + lax.div(step, 2), LEVELS), lax.rem(core + lax.rem(step, 2), 2))
        pl.semaphore_signal(barrier, inc=1, device_id=device, device_id_type=MESH)
        return carry

    lax.fori_loop(1, 2 * LEVELS, greet_column, 0)
    for step in range(1, SIDE):
        for at_chip in (lax.rem(x + step, SIDE) * SIDE + y, x * SIDE + lax.rem(y + step, SIDE)):
            pl.semaphore_signal(barrier, inc=1, device_id=plane_device(at_chip, core), device_id_type=MESH)
    pl.semaphore_wait(barrier, 2 * LEVELS - 1 + 2 * (SIDE - 1))

    def greet_plane():
        for step in range(1, SIDE):
            at_chip = x * SIDE + lax.rem(y + step, SIDE)
            pl.semaphore_signal(line_sem, inc=1, device_id=plane_device(at_chip, core), device_id_type=MESH)
        pl.semaphore_wait(line_sem, SIDE - 1)
        pl.semaphore_signal(core_sem, inc=1, device_id=(seq, z_high * 2 + 1 - core), device_id_type=MESH)
        pl.semaphore_wait(core_sem, 1)

    def near_target(array, index):
        return query.at[index] if array == QUERY else near.at[index, array]

    def send_near(index, array):
        def one(step, carry):
            sign = 1 - 2 * lax.rem(step, 2)
            to = lax.rem(level + LEVELS // 2 + sign * lax.div(step + 1, 2), LEVELS)
            put(
                shards.at[array, :, rows((to * GROUP + index) * HEAD_DIM, HEAD_DIM)],
                near_target(array, index).at[rows(head * SHARD_TOK, SHARD_TOK)],
                send_sem.at[index, array],
                near_sem.at[index, array],
                column_device(to, z_low),
            )
            return carry

        lax.fori_loop(0, LEVELS, one, 0)

    def wait_near(index, array):
        wait_bytes(near_target(array, index), near_sem.at[index, array])

    def send_spread(index, at_core):
        def one(step, carry):
            to = plane_chip(step)
            put(
                near.at[index, at_core, rows(to * PIECE, PIECE)],
                spread[index].at[block],
                spread_send.at[index],
                spread_sem.at[index],
                plane_device(to, at_core),
            )
            return carry

        lax.fori_loop(0, PLANE, one, 0)

    def send_partner(index):
        wait_bytes(spread[index], spread_sem.at[index])
        for rounds in ROUND_SETS[index]:

            def one(step, carry):
                to, at_core = plane_chip(lax.rem(step, PLANE)), lax.div(step, PLANE)
                owner = at_core * PLANE + to
                for round_index in rounds:
                    stage[index][round_index, owner] = spread[index][match_ref[round_index, owner]]
                span = pl.ds(rounds[0], len(rounds))
                put(
                    stage[index].at[span, owner],
                    partner[index].at[span, core, rows(chip * PIECE, PIECE)],
                    partner_send.at[index, rounds[0]],
                    partner_sem.at[index, rounds[0]],
                    plane_device(to, at_core),
                )
                return carry

            lax.fori_loop(0, BLOCKS, one, 0)

    def chunks(ref, turned):
        spans = [slice(start, start + CHUNK) for start in range(0, BLOCK_TOK, CHUNK)]
        return [(ref[KEY, span], turned[:, span]) for span in spans]

    def keep(index, found):
        largest[index], totals[index], mixed[index] = found

    def attend_near(index):
        turned[0] = near[index, VALUE].T
        keep(index, attend_chunks(query[index], chunks(near.at[index], turned.at[0])))

    def attend_partner(index, rounds):
        wait_bytes(partner[index].at[pl.ds(rounds[0], len(rounds))], partner_sem.at[index, rounds[0]])
        pairs = []
        for round_index in rounds:
            turned[round_index] = partner[index][round_index, VALUE].T
            pairs += chunks(partner[index].at[round_index], turned.at[round_index])
        last = rounds[-1] == ROUNDS - 1
        parts = PARTS[index] if last else 1
        width = BLOCK_TOK // parts
        for part in range(parts):
            at = slice(part * width, (part + 1) * width)
            before = largest[index, :, at], totals[index, :, at], mixed[index, :, at]
            found = attend_chunks(query[index, at], pairs, before)
            if not last:
                keep(index, found)
                continue
            done[index, at] = (found[2] / found[1]).T.astype(jnp.bfloat16)
            give(index, part * LEVELS // parts, (part + 1) * LEVELS // parts)

    def give(index, first, end):
        def one(to, carry):
            put(
                done.at[index, rows(to * SHARD_TOK, SHARD_TOK)],
                out_ref.at[:, rows((level * GROUP + index) * HEAD_DIM, HEAD_DIM)],
                out_send.at[index],
                out_sem,
                (block, to),
            )
            return carry

        lax.fori_loop(first, end, one, 0)

    for array in (KEY, VALUE, QUERY):
        wait_bytes(shards.at[array], load_sem.at[array])
    def spread_one(index, array):
        wait_near(index, array)
        send_spread(index, array)

    send_near(0, KEY)
    send_near(0, VALUE)
    send_near(0, QUERY)
    greet_plane()
    spread_one(0, KEY)
    send_near(1, KEY)
    spread_one(0, VALUE)
    send_near(1, VALUE)
    send_partner(0)
    wait_near(0, QUERY)
    send_near(2, KEY)
    attend_near(0)
    spread_one(1, KEY)
    send_near(2, VALUE)
    spread_one(1, VALUE)
    send_near(1, QUERY)
    send_partner(1)
    attend_partner(0, (0, 1))
    spread_one(2, KEY)
    send_near(2, QUERY)
    spread_one(2, VALUE)
    wait_near(1, QUERY)
    attend_near(1)
    send_partner(2)
    attend_partner(1, (0, 1))
    wait_near(2, QUERY)
    attend_near(2)
    attend_partner(2, (0,))
    attend_partner(2, (1,))

    own = core == z_low

    for index in range(GROUP):
        for array in (KEY, VALUE, QUERY):
            @pl.when(own)
            def _():
                wait_bytes(query.at[index, pl.ds(0, (LEVELS - 1) * SHARD_TOK)], send_sem.at[index, array])

            @pl.when(jnp.logical_not(own))
            def _():
                wait_bytes(query.at[index], send_sem.at[index, array])

        wait_bytes(spread[index].at[pl.ds(0, BLOCKS - 1)], spread_send.at[index])
        for rounds in ROUND_SETS[index]:
            wait_bytes(stage[index].at[pl.ds(rounds[0], len(rounds)), pl.ds(0, BLOCKS - 1)], partner_send.at[index, rounds[0]])

        @pl.when(own)
        def _():
            wait_bytes(done.at[index, pl.ds(0, (LEVELS - 1) * SHARD_TOK)], out_send.at[index])

        @pl.when(jnp.logical_not(own))
        def _():
            wait_bytes(done.at[index], out_send.at[index])

    wait_bytes(out_ref, out_sem)


def per_device(query_tokens, key_tokens, value_tokens, matching):
    whole = pl.BlockSpec(memory_space=pl.ANY)
    bf16, f32 = jnp.bfloat16, jnp.float32
    return pl.pallas_call(
        kernel,
        out_shape=jax.ShapeDtypeStruct(query_tokens.shape, bf16),
        in_specs=[pl.BlockSpec(memory_space=pltpu.SMEM), whole, whole, whole],
        out_specs=whole,
        scratch_shapes=[
            pltpu.VMEM((3, SHARD_TOK, WIDTH), bf16),
            pltpu.VMEM((GROUP, 2, BLOCK_TOK, HEAD_DIM), bf16),
            pltpu.VMEM((GROUP, BLOCK_TOK, HEAD_DIM), bf16),
            pltpu.VMEM((GROUP, 1, BLOCK_TOK), f32),
            pltpu.VMEM((GROUP, 1, BLOCK_TOK), f32),
            pltpu.VMEM((GROUP, HEAD_DIM, BLOCK_TOK), f32),
            pltpu.VMEM((GROUP, BLOCK_TOK, HEAD_DIM), bf16),
            pltpu.VMEM((ROUNDS, HEAD_DIM, BLOCK_TOK), bf16),
            *[pltpu.VMEM((BLOCKS, PIECE, HEAD_DIM), bf16)] * GROUP,
            *[pltpu.VMEM((ROUNDS, BLOCKS, PIECE, HEAD_DIM), bf16)] * GROUP,
            *[pltpu.VMEM((ROUNDS, 2, BLOCK_TOK, HEAD_DIM), bf16)] * GROUP,
            pltpu.SemaphoreType.DMA((3,)),
            pltpu.SemaphoreType.DMA((GROUP, 3)),
            pltpu.SemaphoreType.DMA((GROUP, 3)),
            pltpu.SemaphoreType.DMA((GROUP,)),
            pltpu.SemaphoreType.DMA((GROUP,)),
            pltpu.SemaphoreType.DMA((GROUP, ROUNDS)),
            pltpu.SemaphoreType.DMA((GROUP, ROUNDS)),
            pltpu.SemaphoreType.DMA((GROUP,)),
            pltpu.SemaphoreType.DMA,
            pltpu.SemaphoreType.REGULAR,
            pltpu.SemaphoreType.REGULAR,
        ],
        compiler_params=pltpu.CompilerParams(
            collective_id=0, has_side_effects=True, vmem_limit_bytes=56 * 2**20
        ),
    )(matching, query_tokens, key_tokens, value_tokens)


def solution(mesh):
    return jax.shard_map(
        per_device,
        mesh=mesh,
        in_specs=(
            P(("seq", "head"), None),
            P(("seq", "head"), None),
            P(("seq", "head"), None),
            P(),
        ),
        out_specs=P(("seq", "head"), None),
        check_vma=False,
    )
```

```python
import functools
import math

import jax
import jax.numpy as jnp
from jax import lax
from jax.experimental import pallas as pl
from jax.experimental.pallas import tpu as pltpu
from jax.sharding import PartitionSpec as P

HEAD_DIM = 128
ROUNDS = 2
BLOCKS = 32
BLOCK_TOK = 1280
SHARD_TOK = 160
WIDTH = 3072
LEVELS = 8
SIDE = 4
PLANE = SIDE * SIDE
GROUP = WIDTH // HEAD_DIM // LEVELS
PIECE = BLOCK_TOK // PLANE
CHUNK = 256
EXP2_SCALE = math.log2(math.e) / math.sqrt(HEAD_DIM)
MESH = pl.DeviceIdType.MESH
KEY, VALUE, QUERY = range(3)
ROUND_SETS = (((0, 1),), ((0, 1),), ((0,), (1,)))
PARTS = (1, 1, 2)


def rows(start, size, step=None):
    return pl.ds(pl.multiple_of(start, step or size), size)


def attend_chunks(query, pairs, before=None):
    scores = [
        lax.dot_general(keys, query, (((1,), (1,)), ((), ())), preferred_element_type=jnp.float32)
        for keys, _ in pairs
    ]
    largest = functools.reduce(jnp.maximum, [jnp.max(part, axis=0, keepdims=True) for part in scores])
    if before is not None:
        largest = jnp.maximum(largest, before[0])
    totals, mixed = 0.0, 0.0
    for part, (_, values) in zip(scores, pairs):
        weights = jnp.exp2((part - largest) * EXP2_SCALE)
        totals += jnp.sum(weights, axis=0, keepdims=True)
        mixed += jnp.dot(values, weights.astype(jnp.bfloat16), preferred_element_type=jnp.float32)
    if before is not None:
        shrink = jnp.exp2((before[0] - largest) * EXP2_SCALE)
        totals += before[1] * shrink
        mixed += before[2] * shrink
    return largest, totals, mixed


def kernel(match_ref, query_ref, key_ref, value_ref, out_ref, *scratch):
    (shards, near, query, largest, totals, mixed, done, turned) = scratch[:8]
    spread, stage, partner = scratch[8:11], scratch[11:14], scratch[14:17]
    load_sem, send_sem, near_sem, spread_send, spread_sem, partner_send, partner_sem, out_send, out_sem, line_sem, core_sem = scratch[17:]

    seq, head = lax.axis_index("seq"), lax.axis_index("head")
    z_low, chip = lax.div(seq, PLANE), lax.rem(seq, PLANE)
    z_high, core = lax.div(head, 2), lax.rem(head, 2)
    x, y = lax.div(chip, SIDE), lax.rem(chip, SIDE)
    level = z_high * 2 + z_low
    block = core * PLANE + chip

    def column_device(at_level, at_core):
        return lax.rem(at_level, 2) * PLANE + chip, lax.div(at_level, 2) * 2 + at_core

    def plane_device(at_chip, at_core):
        return z_low * PLANE + at_chip, z_high * 2 + at_core

    def plane_chip(step):
        across = lax.rem(lax.div(step, SIDE) + step, SIDE)
        down = lax.rem(step * 3 + lax.div(step, SIDE) * 2, SIDE)
        return lax.rem(x + across, SIDE) * SIDE + lax.rem(y + down, SIDE)

    def put(source, target, send, recv, device):
        here = jnp.logical_and(device[0] == seq, device[1] == head)

        @pl.when(here)
        def _():
            pltpu.make_async_copy(source, target, recv).start()

        @pl.when(jnp.logical_not(here))
        def _():
            pltpu.make_async_remote_copy(source, target, send, recv, device_id=device, device_id_type=MESH).start()

    def wait_bytes(ref, sem):
        pltpu.make_async_copy(ref, ref, sem).wait()

    for array, ref in ((KEY, key_ref), (VALUE, value_ref), (QUERY, query_ref)):
        pltpu.make_async_copy(ref, shards.at[array], load_sem.at[array]).start()

    barrier = pltpu.get_barrier_semaphore()

    def greet_column(step, carry):
        device = column_device(lax.rem(level + lax.div(step, 2), LEVELS), lax.rem(core + lax.rem(step, 2), 2))
        pl.semaphore_signal(barrier, inc=1, device_id=device, device_id_type=MESH)
        return carry

    lax.fori_loop(1, 2 * LEVELS, greet_column, 0)
    for step in range(1, SIDE):
        for at_chip in (lax.rem(x + step, SIDE) * SIDE + y, x * SIDE + lax.rem(y + step, SIDE)):
            pl.semaphore_signal(barrier, inc=1, device_id=plane_device(at_chip, core), device_id_type=MESH)
    pl.semaphore_wait(barrier, 2 * LEVELS - 1 + 2 * (SIDE - 1))

    def greet_plane():
        for step in range(1, SIDE):
            at_chip = x * SIDE + lax.rem(y + step, SIDE)
            pl.semaphore_signal(line_sem, inc=1, device_id=plane_device(at_chip, core), device_id_type=MESH)
        pl.semaphore_wait(line_sem, SIDE - 1)
        pl.semaphore_signal(core_sem, inc=1, device_id=(seq, z_high * 2 + 1 - core), device_id_type=MESH)
        pl.semaphore_wait(core_sem, 1)

    def near_target(array, index):
        return query.at[index] if array == QUERY else near.at[index, array]

    def send_near(index, array):
        def one(step, carry):
            sign = 1 - 2 * lax.rem(step, 2)
            to = lax.rem(level + LEVELS // 2 + sign * lax.div(step + 1, 2), LEVELS)
            put(
                shards.at[array, :, rows((to * GROUP + index) * HEAD_DIM, HEAD_DIM)],
                near_target(array, index).at[rows(head * SHARD_TOK, SHARD_TOK)],
                send_sem.at[index, array],
                near_sem.at[index, array],
                column_device(to, z_low),
            )
            return carry

        lax.fori_loop(0, LEVELS, one, 0)

    def wait_near(index, array):
        wait_bytes(near_target(array, index), near_sem.at[index, array])

    def send_spread(index, at_core):
        def one(step, carry):
            to = plane_chip(step)
            put(
                near.at[index, at_core, rows(to * PIECE, PIECE)],
                spread[index].at[block],
                spread_send.at[index],
                spread_sem.at[index],
                plane_device(to, at_core),
            )
            return carry

        lax.fori_loop(0, PLANE, one, 0)

    def send_partner(index):
        wait_bytes(spread[index], spread_sem.at[index])
        for rounds in ROUND_SETS[index]:

            def one(step, carry):
                to, at_core = plane_chip(lax.rem(step, PLANE)), lax.div(step, PLANE)
                owner = at_core * PLANE + to
                for round_index in rounds:
                    stage[index][round_index, owner] = spread[index][match_ref[round_index, owner]]
                span = pl.ds(rounds[0], len(rounds))
                put(
                    stage[index].at[span, owner],
                    partner[index].at[span, core, rows(chip * PIECE, PIECE)],
                    partner_send.at[index, rounds[0]],
                    partner_sem.at[index, rounds[0]],
                    plane_device(to, at_core),
                )
                return carry

            lax.fori_loop(0, BLOCKS, one, 0)

    def chunks(ref, turned):
        spans = [slice(start, start + CHUNK) for start in range(0, BLOCK_TOK, CHUNK)]
        return [(ref[KEY, span], turned[:, span]) for span in spans]

    def keep(index, found):
        largest[index], totals[index], mixed[index] = found

    def attend_near(index):
        turned[0] = near[index, VALUE].T
        keep(index, attend_chunks(query[index], chunks(near.at[index], turned.at[0])))

    def attend_partner(index, rounds):
        wait_bytes(partner[index].at[pl.ds(rounds[0], len(rounds))], partner_sem.at[index, rounds[0]])
        pairs = []
        for round_index in rounds:
            turned[round_index] = partner[index][round_index, VALUE].T
            pairs += chunks(partner[index].at[round_index], turned.at[round_index])
        last = rounds[-1] == ROUNDS - 1
        parts = PARTS[index] if last else 1
        width = BLOCK_TOK // parts
        for part in range(parts):
            at = slice(part * width, (part + 1) * width)
            before = largest[index, :, at], totals[index, :, at], mixed[index, :, at]
            found = attend_chunks(query[index, at], pairs, before)
            if not last:
                keep(index, found)
                continue
            done[index, at] = (found[2] / found[1]).T.astype(jnp.bfloat16)
            give(index, part * LEVELS // parts, (part + 1) * LEVELS // parts)

    def give(index, first, end):
        def one(to, carry):
            put(
                done.at[index, rows(to * SHARD_TOK, SHARD_TOK)],
                out_ref.at[:, rows((level * GROUP + index) * HEAD_DIM, HEAD_DIM)],
                out_send.at[index],
                out_sem,
                (block, to),
            )
            return carry

        lax.fori_loop(first, end, one, 0)

    for array in (KEY, VALUE, QUERY):
        wait_bytes(shards.at[array], load_sem.at[array])
    def spread_one(index, array):
        wait_near(index, array)
        send_spread(index, array)

    send_near(0, KEY)
    send_near(0, VALUE)
    send_near(0, QUERY)
    greet_plane()
    spread_one(0, KEY)
    send_near(1, KEY)
    spread_one(0, VALUE)
    send_near(1, VALUE)
    send_partner(0)
    wait_near(0, QUERY)
    send_near(2, KEY)
    attend_near(0)
    spread_one(1, KEY)
    send_near(2, VALUE)
    spread_one(1, VALUE)
    send_near(1, QUERY)
    send_partner(1)
    attend_partner(0, (0, 1))
    spread_one(2, KEY)
    send_near(2, QUERY)
    spread_one(2, VALUE)
    wait_near(1, QUERY)
    attend_near(1)
    send_partner(2)
    attend_partner(1, (0, 1))
    wait_near(2, QUERY)
    attend_near(2)
    attend_partner(2, (0,))
    attend_partner(2, (1,))

    own = core == z_low

    for index in range(GROUP):
        for array in (KEY, VALUE, QUERY):
            @pl.when(own)
            def _():
                wait_bytes(query.at[index, pl.ds(0, (LEVELS - 1) * SHARD_TOK)], send_sem.at[index, array])

            @pl.when(jnp.logical_not(own))
            def _():
                wait_bytes(query.at[index], send_sem.at[index, array])

        wait_bytes(spread[index].at[pl.ds(0, BLOCKS - 1)], spread_send.at[index])
        for rounds in ROUND_SETS[index]:
            wait_bytes(stage[index].at[pl.ds(rounds[0], len(rounds)), pl.ds(0, BLOCKS - 1)], partner_send.at[index, rounds[0]])

        @pl.when(own)
        def _():
            wait_bytes(done.at[index, pl.ds(0, (LEVELS - 1) * SHARD_TOK)], out_send.at[index])

        @pl.when(jnp.logical_not(own))
        def _():
            wait_bytes(done.at[index], out_send.at[index])

    wait_bytes(out_ref, out_sem)


def per_device(query_tokens, key_tokens, value_tokens, matching):
    whole = pl.BlockSpec(memory_space=pl.ANY)
    bf16, f32 = jnp.bfloat16, jnp.float32
    return pl.pallas_call(
        kernel,
        out_shape=jax.ShapeDtypeStruct(query_tokens.shape, bf16),
        in_specs=[pl.BlockSpec(memory_space=pltpu.SMEM), whole, whole, whole],
        out_specs=whole,
        scratch_shapes=[
            pltpu.VMEM((3, SHARD_TOK, WIDTH), bf16),
            pltpu.VMEM((GROUP, 2, BLOCK_TOK, HEAD_DIM), bf16),
            pltpu.VMEM((GROUP, BLOCK_TOK, HEAD_DIM), bf16),
            pltpu.VMEM((GROUP, 1, BLOCK_TOK), f32),
            pltpu.VMEM((GROUP, 1, BLOCK_TOK), f32),
            pltpu.VMEM((GROUP, HEAD_DIM, BLOCK_TOK), f32),
            pltpu.VMEM((GROUP, BLOCK_TOK, HEAD_DIM), bf16),
            pltpu.VMEM((ROUNDS, HEAD_DIM, BLOCK_TOK), bf16),
            *[pltpu.VMEM((BLOCKS, PIECE, HEAD_DIM), bf16)] * GROUP,
            *[pltpu.VMEM((ROUNDS, BLOCKS, PIECE, HEAD_DIM), bf16)] * GROUP,
            *[pltpu.VMEM((ROUNDS, 2, BLOCK_TOK, HEAD_DIM), bf16)] * GROUP,
            pltpu.SemaphoreType.DMA((3,)),
            pltpu.SemaphoreType.DMA((GROUP, 3)),
            pltpu.SemaphoreType.DMA((GROUP, 3)),
            pltpu.SemaphoreType.DMA((GROUP,)),
            pltpu.SemaphoreType.DMA((GROUP,)),
            pltpu.SemaphoreType.DMA((GROUP, ROUNDS)),
            pltpu.SemaphoreType.DMA((GROUP, ROUNDS)),
            pltpu.SemaphoreType.DMA((GROUP,)),
            pltpu.SemaphoreType.DMA,
            pltpu.SemaphoreType.REGULAR,
            pltpu.SemaphoreType.REGULAR,
        ],
        compiler_params=pltpu.CompilerParams(
            collective_id=0, has_side_effects=True, vmem_limit_bytes=48 * 2**20
        ),
    )(matching, query_tokens, key_tokens, value_tokens)


def solution(mesh):
    return jax.shard_map(
        per_device,
        mesh=mesh,
        in_specs=(
            P(("seq", "head"), None),
            P(("seq", "head"), None),
            P(("seq", "head"), None),
            P(),
        ),
        out_specs=P(("seq", "head"), None),
        check_vma=False,
    )
```
